32 devices in a mesh: seg: 8 (over z, y), op: 4 (over x, core).
Axes of the slice: x: 2, y: 2, z: 4, core: 2. Of those that a mesh axis runs over, the one named last changes fastest.
Arguments:
- label_map: int32 [8, 16], P('seg'), may hold values from 0 to 15, each once within a row
- site_blocks: float32 [8, 16, 128, 128], P('seg'), may hold values from -0.25 to 1.25
- left_ops: bfloat16 [48, 16, 128, 128], P('op'), may hold values from -0.5 to 0.5
- right_ops: bfloat16 [8, 48, 16, 128, 128], P('seg', 'op'), may hold values from -0.078125 to 0.078125
- wavefunction: bfloat16 [8, 16, 128, 128], P('seg', 'op'), may hold values from -72 to 72
Outputs:
- ham_psi: bfloat16 [8, 16, 128, 128], P('seg', 'op')
- ham_squared_psi: bfloat16 [8, 16, 128, 128], P('seg', 'op')
The draws below stay inside these ranges and needn't reach their ends.
Inputs may be any that keep to these rules, and one draw needn't show every extreme that they name: Each row of label_map is a permutation of 0 to 15.
All inputs are finite; a program needn't handle non-finite values.
Results may differ from the reference program's by a relative error of at most 0.022.
Values may be sent and summed in bfloat16 or wider, within the bound.
A program may use at most 128 MiB of HBM per device.

```python
import math
import jax
import jax.numpy as jnp
from jax import lax

NB = 16
BS = 128
OPS = 48
NSEG = 8


def draw_site_blocks(key, part):
    array_shape = (NSEG, NB, BS, BS)
    fluctuation = jnp.clip(jax.random.normal(key, array_shape, jnp.float32), -4.0, 4.0)
    unit_diagonal = (jnp.arange(BS)[:, None] == jnp.arange(BS)[None, :]).astype(jnp.float32)
    return (unit_diagonal + 0.25 * fluctuation / math.sqrt(BS)) / math.sqrt(1.0625)


def draw_wavefunction(key, part):
    key_list = jax.random.split(key, 4)
    array_shape = (NSEG, NB, BS, BS)
    base_vals = jnp.clip(jax.random.normal(key_list[0], array_shape, jnp.float32), -4.0, 4.0)
    row_scale = jnp.exp(jax.random.uniform(key_list[1], (NSEG, NB, BS, 1), jnp.float32, math.log(0.4), math.log(4.0)))
    col_scale = jnp.exp(jax.random.uniform(key_list[2], (NSEG, NB, 1, BS), jnp.float32, math.log(0.4), math.log(4.0)))
    rising = jnp.power(3.0, jnp.arange(NB, dtype=jnp.float32) / max(NB - 1, 1))[None, :, None, None]
    jitter = jax.random.uniform(key_list[3], (NSEG, NB, 1, 1), jnp.float32, 0.8, 1.25)
    return (0.3 * base_vals * row_scale * col_scale * rising * jitter).astype(jnp.bfloat16)


def shard_levels(key, dims, shards, least, largest):
    level = 1.0
    for axis_at, parts in shards:
        heights = jax.random.uniform(jax.random.fold_in(jax.random.fold_in(key, 6), axis_at), (parts,), jnp.float32, least / len(shards), largest / len(shards))
        level = level * jnp.repeat(jnp.exp(heights), dims[axis_at] // parts).reshape((-1,) + (1,) * (len(dims) - 1 - axis_at))
    return level


def scatter_about(key, dims, deviation, bound, cuts=(), held_as=jnp.bfloat16):
    values = deviation * jax.random.normal(key, dims, jnp.float32)
    if cuts:
        values = values * shard_levels(key, dims, cuts, -0.22, 0.18)
    return jnp.clip(values, -bound, bound).astype(held_as)


def setup_inputs(seed: int = 0) -> dict:
    key_of = jax.random.split(jax.random.key(seed), 6)
    label_map = jax.vmap(lambda own: jax.random.permutation(own, NB))(jax.random.split(key_of[0], NSEG)).reshape((NSEG, NB)).astype(jnp.int32)
    site_blocks = draw_site_blocks(jax.random.fold_in(key_of[5], 71), 0)
    left_ops = scatter_about(key_of[2], (OPS, NB, BS, BS), BS ** -0.5, 0.5, ((0, 4),))
    right_ops = scatter_about(key_of[3], (NSEG, OPS, NB, BS, BS), (BS * OPS) ** -0.5, 0.078125, ((0, 8), (1, 4)))
    wavefunction = draw_wavefunction(jax.random.fold_in(key_of[5], 71), 0)
    return {"label_map": label_map, "site_blocks": site_blocks, "left_ops": left_ops, "right_ops": right_ops, "wavefunction": wavefunction}


def reference(label_map, site_blocks, left_ops, right_ops, wavefunction):
    highest = lax.Precision.HIGHEST
    identity = jnp.eye(BS, dtype=jnp.float32)

    def advance(state_pair, inputs):
        blocks, labels = state_pair
        site_seg, map_seg = inputs
        picked = jnp.take(site_seg, labels, axis=0)
        new_blocks = jnp.einsum('qij,qjk->qik', blocks, picked, precision=highest)
        new_labels = jnp.take(map_seg, labels).astype(jnp.int32)
        return ((new_blocks, new_labels), (blocks, labels))
    initial = (jnp.broadcast_to(identity, (NB, BS, BS)).astype(jnp.float32), jnp.arange(NB, dtype=jnp.int32))
    final_state, (prefix, labels) = lax.scan(advance, initial, (site_blocks, label_map.astype(jnp.int32)))
    left_wide = left_ops.astype(jnp.float32)

    def segment(inputs):
        seg_prefix, seg_labels, seg_right, seg_psi = inputs
        inverse = jnp.argsort(seg_labels).astype(jnp.int32)
        inner_prod = jnp.einsum('kqjl,qlm->kqjm', left_wide, seg_prefix, precision=highest)
        environ = jnp.einsum('qji,kqjm->kqim', seg_prefix, inner_prod, precision=highest)
        environ = jnp.take(environ, inverse, axis=1).astype(jnp.bfloat16)
        env_wide = environ.astype(jnp.float32)
        right_wide = seg_right.astype(jnp.float32)

        def apply_ham(vector):
            half_prod = jnp.einsum('kpij,pjl->kpil', env_wide, vector.astype(jnp.float32)).astype(jnp.bfloat16)
            return jnp.einsum('kpil,kpml->pim', half_prod.astype(jnp.float32), right_wide)
        hpsi_sum = apply_ham(seg_psi)
        scale_fac = lax.rsqrt(jnp.sum(hpsi_sum * hpsi_sum) / (NB * BS * BS) + 1e-06)
        unit_vec = (hpsi_sum * scale_fac).astype(jnp.bfloat16)
        second = apply_ham(unit_vec).astype(jnp.bfloat16)
        return (hpsi_sum.astype(jnp.bfloat16), second)
    ham_psi, ham_squared_psi = lax.map(segment, (prefix, labels, right_ops, wavefunction))
    return (ham_psi, ham_squared_psi)
```

```python
import functools

import jax
import jax.numpy as jnp
from jax import lax
from jax.experimental import pallas as pl
from jax.experimental.pallas import tpu as pltpu
from jax.sharding import PartitionSpec as P

MESH = pl.DeviceIdType.MESH
F32 = jnp.float32
BF16 = jnp.bfloat16
NT = (((1,), (1,)), ((), ()))
TN = (((0,), (0,)), ((), ()))


def mixed(index, off, count):
    out = index * 0
    bit = 1
    while bit < count:
        digit = (index // bit) % 2
        out = out + bit * ((1 - digit) if off & bit else digit)
        bit *= 2
    return out


def split(value):
    high = value.astype(BF16)
    return high, (value - high.astype(F32)).astype(BF16)


def mm(a, b):
    return jnp.dot(a, b, preferred_element_type=F32)


def kernel(
    segs, groups, label_ref, site_hbm, left_hbm, right_hbm, wave_hbm, out1_ref, out2_ref,
    site, left, right, wave, lab_own, lab_all, lab_smem, sector_to, sector_from,
    prefix, step_hi, step_lo, step_out, hpsi, z_own, zs1, zr1, zs2, zr2,
    load_sem, smem_sem, lab_send, lab_recv, wave_send, wave_recv, chain_send, chain_recv,
    pre_send, pre_recv, z1_send, z1_recv, h_send, h_recv, z2_send, z2_recv,
):
    seg = lax.axis_index("seg")
    me = lax.axis_index("op")
    sectors, block_len = prefix.shape[0], prefix.shape[1]
    per = sectors // groups
    ops = left.shape[0]
    first = me * per

    loads = [
        pltpu.make_async_copy(site_hbm.at[0], site, load_sem.at[0]),
        pltpu.make_async_copy(wave_hbm.at[0], wave.at[pl.ds(first, per)], load_sem.at[1]),
        pltpu.make_async_copy(left_hbm, left, load_sem.at[2]),
        pltpu.make_async_copy(right_hbm.at[0], right, load_sem.at[3]),
    ]
    for load in loads:
        load.start()
    lab_own[...] = jnp.zeros_like(lab_own)
    lab_own[0:1, 0:sectors] = label_ref[...]
    lab_all[seg] = lab_own[...]

    barrier = pltpu.get_barrier_semaphore()
    for off in range(1, groups):
        pl.semaphore_signal(
            barrier, inc=1, device_id={"op": mixed(me, off, groups)}, device_id_type=MESH
        )
    for off in range(1, segs):
        pl.semaphore_signal(
            barrier, inc=1, device_id={"seg": (seg + off) % segs}, device_id_type=MESH
        )
    pl.semaphore_wait(barrier, groups + segs - 2)

    def to_op(src, dst, send, recv, off):
        return pltpu.make_async_remote_copy(
            src_ref=src, dst_ref=dst, send_sem=send, recv_sem=recv,
            device_id={"op": mixed(me, off, groups)}, device_id_type=MESH,
        )

    def lab_copy(off, source):
        return pltpu.make_async_remote_copy(
            src_ref=lab_own, dst_ref=lab_all.at[source], send_sem=lab_send.at[off - 1],
            recv_sem=lab_recv.at[off - 1],
            device_id={"seg": (seg + off) % segs}, device_id_type=MESH,
        )

    for off in range(1, segs):
        lab_copy(off, seg).start()

    loads[1].wait()

    def wave_copy(off, owner):
        rows = pl.ds(owner * per, per)
        return to_op(
            wave.at[rows], wave.at[rows], wave_send.at[off - 1], wave_recv.at[off - 1], off
        )

    for off in range(1, groups):
        wave_copy(off, me).start()

    for off in range(1, segs):
        lab_copy(off, (seg + segs - off) % segs).wait_recv()
    to_smem = pltpu.make_async_copy(lab_all, lab_smem, smem_sem)
    to_smem.start()
    to_smem.wait()

    def reached(q, _):
        p = lax.fori_loop(0, seg, lambda s, p: lab_smem[s, 0, p], q)
        sector_to[q] = jnp.clip(p, 0, sectors - 1)
        return 0

    lax.fori_loop(0, sectors, reached, 0)

    loads[0].wait()
    for j in range(per):
        high, low = split(site[sector_to[first + j]])
        step_hi[j] = high
        step_lo[j] = low

    def chain_copy(j):
        return pltpu.make_async_remote_copy(
            src_ref=step_out.at[j], dst_ref=prefix.at[first + j], send_sem=chain_send.at[j],
            recv_sem=chain_recv.at[j],
            device_id={"seg": (seg + 1) % segs}, device_id_type=MESH,
        )

    def prefix_copy(off, j, owner):
        block = prefix.at[owner * per + j]
        return to_op(block, block, pre_send.at[off - 1, j], pre_recv.at[off - 1, j], off)

    row = lax.broadcasted_iota(jnp.int32, (block_len, block_len), 0)
    col = lax.broadcasted_iota(jnp.int32, (block_len, block_len), 1)
    for j in range(per):

        @pl.when(seg == 0)
        def _():
            prefix[first + j] = jnp.where(row == col, 1.0, 0.0).astype(BF16)

        @pl.when(seg > 0)
        def _():
            chain_copy(j).wait_recv()

        @pl.when(seg < segs - 1)
        def _():
            block = prefix[first + j]
            step_out[j] = (mm(block, step_hi[j]) + mm(block, step_lo[j])).astype(BF16)
            chain_copy(j).start()

        for off in range(1, groups):
            prefix_copy(off, j, me).start()

    def found(p, _):
        def look(q, at):
            return jnp.where(sector_to[q] == p, q, at)

        sector_from[p] = lax.fori_loop(0, sectors, look, jnp.int32(0))
        return 0

    lax.fori_loop(0, sectors, found, 0)

    for off in range(1, groups):
        wave_copy(off, mixed(me, off, groups)).wait_recv()
        for j in range(per):
            prefix_copy(off, j, mixed(me, off, groups)).wait_recv()
    loads[2].wait()
    loads[3].wait()

    def terms(q, p, vector):
        inner = mm(prefix[q], vector).astype(BF16)
        total = jnp.zeros((block_len, block_len), F32)
        for k in range(0, ops, 2):
            pair = [k] if k + 1 == ops else [k, k + 1]
            half = [mm(left[i, q], inner).astype(BF16) for i in pair]
            other = [right[i, p] for i in pair]
            total += lax.dot_general(
                jnp.concatenate(half, axis=1), jnp.concatenate(other, axis=1), NT,
                preferred_element_type=F32,
            )
        return total

    def z1_copy(off, j):
        return to_op(
            zs1.at[off - 1, j], zr1.at[off - 1, j],
            z1_send.at[off - 1, j], z1_recv.at[off - 1, j], off,
        )

    def z2_copy(off, j):
        return to_op(
            zs2.at[off - 1, j], zr2.at[off - 1, j],
            z2_send.at[off - 1, j], z2_recv.at[off - 1, j], off,
        )

    for off in range(groups):
        owner = mixed(me, off, groups)

        def first_step(j, _):
            q = owner * per + j
            p = sector_to[q]
            total = terms(q, p, wave[p])
            if off:
                zs1[off - 1, j] = total.astype(BF16)
                z1_copy(off, j).start()
            else:
                z_own[j] = total
            return 0

        lax.fori_loop(0, per, first_step, 0)

    def back(q, total):
        high, low = split(total)
        block = prefix[q]
        return lax.dot_general(block, high, TN, preferred_element_type=F32) + lax.dot_general(
            block, low, TN, preferred_element_type=F32
        )

    def h_copy(off, j, owner):
        block = hpsi.at[owner * per + j]
        return to_op(block, block, h_send.at[off - 1, j], h_recv.at[off - 1, j], off)

    for j in range(per):
        total = z_own[j]
        for off in range(1, groups):
            z1_copy(off, j).wait_recv()
            total += zr1[off - 1, j].astype(F32)
        hpsi[first + j] = back(first + j, total).astype(BF16)
        for off in range(1, groups):
            h_copy(off, j, me).start()
    for j in range(per):
        for off in range(1, groups):
            h_copy(off, j, mixed(me, off, groups)).wait_recv()

    for off in list(range(1, groups)) + [0]:
        owner = mixed(me, off, groups)

        def second_step(j, _):
            p = owner * per + j
            q = sector_from[p]
            total = terms(q, p, hpsi[q])
            if off:
                zs2[off - 1, j] = total.astype(BF16)
                z2_copy(off, j).start()
            else:
                z_own[j] = total
            return 0

        lax.fori_loop(0, per, second_step, 0)

    def add_squares(q, sums):
        block = hpsi[q].astype(F32)
        return sums + block * block

    squares = lax.fori_loop(0, sectors, add_squares, jnp.zeros((block_len, block_len), F32))
    entries = sectors * block_len * block_len
    scale = lax.rsqrt(jnp.sum(squares, keepdims=True) / entries + 1e-06)
    for j in range(per):
        out1_ref[0, j] = hpsi[sector_from[first + j]]
    for j in range(per):
        total = z_own[j]
        for off in range(1, groups):
            z2_copy(off, j).wait_recv()
            total += zr2[off - 1, j].astype(F32)
        out2_ref[0, j] = (back(sector_from[first + j], total) * scale).astype(BF16)

    for off in range(1, segs):
        lab_copy(off, seg).wait_send()
    for off in range(1, groups):
        wave_copy(off, me).wait_send()
        for j in range(per):
            prefix_copy(off, j, me).wait_send()
            z1_copy(off, j).wait_send()
            h_copy(off, j, me).wait_send()
            z2_copy(off, j).wait_send()

    @pl.when(seg < segs - 1)
    def _():
        for j in range(per):
            chain_copy(j).wait_send()


def on_device(label_map, site_blocks, left_ops, right_ops, wavefunction):
    segs, groups = lax.axis_size("seg"), lax.axis_size("op")
    sectors, n = site_blocks.shape[1], site_blocks.shape[2]
    ops = left_ops.shape[0]
    per = sectors // groups
    dma = pltpu.SemaphoreType.DMA
    peers = groups - 1
    blocks = lambda *lead, dtype=BF16: pltpu.VMEM(lead + (n, n), dtype)
    out = jax.ShapeDtypeStruct((1, per, n, n), BF16)
    vmem = pl.BlockSpec(memory_space=pltpu.VMEM)
    hbm = pl.BlockSpec(memory_space=pl.ANY)
    return pl.pallas_call(
        functools.partial(kernel, segs, groups),
        out_shape=(out, out),
        in_specs=[vmem, hbm, hbm, hbm, hbm],
        out_specs=(vmem, vmem),
        scratch_shapes=[
            blocks(sectors, dtype=F32), blocks(ops, sectors), blocks(ops, sectors),
            blocks(sectors),
            pltpu.VMEM((8, 128), jnp.int32), pltpu.VMEM((segs, 8, 128), jnp.int32),
            pltpu.SMEM((segs, 8, 128), jnp.int32),
            pltpu.SMEM((sectors,), jnp.int32), pltpu.SMEM((sectors,), jnp.int32),
            blocks(sectors), blocks(per), blocks(per), blocks(per), blocks(sectors),
            blocks(per, dtype=F32),
            blocks(peers, per), blocks(peers, per), blocks(peers, per), blocks(peers, per),
            dma((4,)), dma, dma((segs - 1,)), dma((segs - 1,)), dma((peers,)), dma((peers,)),
            dma((per,)), dma((per,)),
            dma((peers, per)), dma((peers, per)), dma((peers, per)), dma((peers, per)),
            dma((peers, per)), dma((peers, per)), dma((peers, per)), dma((peers, per)),
        ],
        compiler_params=pltpu.CompilerParams(
            collective_id=0, has_side_effects=True, vmem_limit_bytes=56 * 1024 * 1024
        ),
    )(label_map, site_blocks, left_ops, right_ops, wavefunction)


def solution(mesh):
    in_specs = (
        P("seg", None),
        P("seg", None, None, None),
        P("op", None, None, None),
        P("seg", "op", None, None, None),
        P("seg", "op", None, None),
    )
    out_specs = (P("seg", "op", None, None), P("seg", "op", None, None))
    return jax.shard_map(
        on_device, mesh=mesh, in_specs=in_specs, out_specs=out_specs, check_vma=False
    )
```

```python
import functools

import jax
import jax.numpy as jnp
from jax import lax
from jax.experimental import pallas as pl
from jax.experimental.pallas import tpu as pltpu
from jax.sharding import PartitionSpec as P

MESH = pl.DeviceIdType.MESH
F32 = jnp.float32
BF16 = jnp.bfloat16
NT = (((1,), (1,)), ((), ()))
TN = (((0,), (0,)), ((), ()))


def mixed(index, off, count):
    out = index * 0
    bit = 1
    while bit < count:
        digit = (index // bit) % 2
        out = out + bit * ((1 - digit) if off & bit else digit)
        bit *= 2
    return out


def split(value):
    high = value.astype(BF16)
    return high, (value - high.astype(F32)).astype(BF16)


def mm(a, b):
    return jnp.dot(a, b, preferred_element_type=F32)


def kernel(
    segs, groups, label_ref, site_hbm, left_hbm, right_hbm, wave_hbm, out1_ref, out2_ref,
    site, left, right, wave, lab_own, lab_all, lab_smem, sector_to, sector_from,
    prefix, step_hi, step_lo, step_out, hpsi, z_own, zs1, zr1, zs2, zr2,
    load_sem, smem_sem, lab_send, lab_recv, wave_send, wave_recv, chain_send, chain_recv,
    pre_send, pre_recv, z1_send, z1_recv, h_send, h_recv, z2_send, z2_recv,
):
    seg = lax.axis_index("seg")
    me = lax.axis_index("op")
    sectors, block_len = prefix.shape[0], prefix.shape[1]
    per = sectors // groups
    ops = left.shape[0]
    first = me * per

    loads = [
        pltpu.make_async_copy(site_hbm.at[0], site, load_sem.at[0]),
        pltpu.make_async_copy(wave_hbm.at[0], wave.at[pl.ds(first, per)], load_sem.at[1]),
        pltpu.make_async_copy(left_hbm, left, load_sem.at[2]),
        pltpu.make_async_copy(right_hbm.at[0], right, load_sem.at[3]),
    ]
    for load in loads:
        load.start()
    lab_own[...] = jnp.zeros_like(lab_own)
    lab_own[0:1, 0:sectors] = label_ref[...]
    lab_all[seg] = lab_own[...]

    barrier = pltpu.get_barrier_semaphore()
    for off in range(1, groups):
        pl.semaphore_signal(
            barrier, inc=1, device_id={"op": mixed(me, off, groups)}, device_id_type=MESH
        )
    for off in range(1, segs):
        pl.semaphore_signal(
            barrier, inc=1, device_id={"seg": (seg + off) % segs}, device_id_type=MESH
        )
    pl.semaphore_wait(barrier, groups + segs - 2)

    def to_op(src, dst, send, recv, off):
        return pltpu.make_async_remote_copy(
            src_ref=src, dst_ref=dst, send_sem=send, recv_sem=recv,
            device_id={"op": mixed(me, off, groups)}, device_id_type=MESH,
        )

    def lab_copy(off, source):
        return pltpu.make_async_remote_copy(
            src_ref=lab_own, dst_ref=lab_all.at[source], send_sem=lab_send.at[off - 1],
            recv_sem=lab_recv.at[off - 1],
            device_id={"seg": (seg + off) % segs}, device_id_type=MESH,
        )

    for off in range(1, segs):
        lab_copy(off, seg).start()

    loads[1].wait()

    def wave_copy(off, owner):
        rows = pl.ds(owner * per, per)
        return to_op(
            wave.at[rows], wave.at[rows], wave_send.at[off - 1], wave_recv.at[off - 1], off
        )

    for off in range(1, groups):
        wave_copy(off, me).start()

    for off in range(1, segs):
        lab_copy(off, (seg + segs - off) % segs).wait_recv()
    to_smem = pltpu.make_async_copy(lab_all, lab_smem, smem_sem)
    to_smem.start()
    to_smem.wait()

    def reached(q, _):
        p = lax.fori_loop(0, seg, lambda s, p: lab_smem[s, 0, p], q)
        sector_to[q] = jnp.clip(p, 0, sectors - 1)
        return 0

    lax.fori_loop(0, sectors, reached, 0)

    loads[0].wait()
    for j in range(per):
        high, low = split(site[sector_to[first + j]])
        step_hi[j] = high
        step_lo[j] = low

    def chain_copy(j):
        return pltpu.make_async_remote_copy(
            src_ref=step_out.at[j], dst_ref=prefix.at[first + j], send_sem=chain_send.at[j],
            recv_sem=chain_recv.at[j],
            device_id={"seg": (seg + 1) % segs}, device_id_type=MESH,
        )

    def prefix_copy(off, j, owner):
        block = prefix.at[owner * per + j]
        return to_op(block, block, pre_send.at[off - 1, j], pre_recv.at[off - 1, j], off)

    row = lax.broadcasted_iota(jnp.int32, (block_len, block_len), 0)
    col = lax.broadcasted_iota(jnp.int32, (block_len, block_len), 1)
    for j in range(per):

        @pl.when(seg == 0)
        def _():
            prefix[first + j] = jnp.where(row == col, 1.0, 0.0).astype(BF16)

        @pl.when(seg > 0)
        def _():
            chain_copy(j).wait_recv()

        @pl.when(seg < segs - 1)
        def _():
            block = prefix[first + j]
            step_out[j] = (mm(block, step_hi[j]) + mm(block, step_lo[j])).astype(BF16)
            chain_copy(j).start()

        for off in range(1, groups):
            prefix_copy(off, j, me).start()

    def found(p, _):
        def look(q, at):
            return jnp.where(sector_to[q] == p, q, at)

        sector_from[p] = lax.fori_loop(0, sectors, look, jnp.int32(0))
        return 0

    lax.fori_loop(0, sectors, found, 0)

    for off in range(1, groups):
        wave_copy(off, mixed(me, off, groups)).wait_recv()
    loads[2].wait()
    loads[3].wait()

    def terms(q, p, vector):
        inner = mm(prefix[q], vector).astype(BF16)
        stacked = left[:, q].reshape(ops * block_len, block_len)
        half = mm(stacked, inner).astype(BF16).reshape(ops, block_len, block_len)
        return lax.dot_general(
            jnp.concatenate([half[k] for k in range(ops)], axis=1),
            jnp.concatenate([right[k, p] for k in range(ops)], axis=1),
            NT, preferred_element_type=F32,
        )

    def z1_copy(off, j):
        return to_op(
            zs1.at[off - 1, j], zr1.at[off - 1, j],
            z1_send.at[off - 1, j], z1_recv.at[off - 1, j], off,
        )

    def z2_copy(off, j):
        return to_op(
            zs2.at[off - 1, j], zr2.at[off - 1, j],
            z2_send.at[off - 1, j], z2_recv.at[off - 1, j], off,
        )

    for j in range(per):
        p = sector_to[first + j]
        z_own[j] = terms(first + j, p, wave[p])
    for off in range(1, groups):
        for j in range(per):
            prefix_copy(off, j, mixed(me, off, groups)).wait_recv()
    for off in range(1, groups):
        owner = mixed(me, off, groups)
        for j in range(0, per, 2):
            totals = []
            for i in range(j, j + 2):
                q = owner * per + i
                p = sector_to[q]
                totals.append(terms(q, p, wave[p]))
            for i in range(j, j + 2):
                zs1[off - 1, i] = totals[i - j].astype(BF16)
                z1_copy(off, i).start()

    def back(q, total):
        high, low = split(total)
        block = prefix[q]
        return lax.dot_general(block, high, TN, preferred_element_type=F32) + lax.dot_general(
            block, low, TN, preferred_element_type=F32
        )

    def h_copy(off, j, owner):
        block = hpsi.at[owner * per + j]
        return to_op(block, block, h_send.at[off - 1, j], h_recv.at[off - 1, j], off)

    for j in range(per):
        total = z_own[j]
        for off in range(1, groups):
            z1_copy(off, j).wait_recv()
            total += zr1[off - 1, j].astype(F32)
        hpsi[first + j] = back(first + j, total).astype(BF16)
        for off in range(1, groups):
            h_copy(off, j, me).start()
    for j in range(per):
        for off in range(1, groups):
            h_copy(off, j, mixed(me, off, groups)).wait_recv()

    for off in list(range(1, groups)) + [0]:
        owner = mixed(me, off, groups)

        for j in range(0, per, 2):
            totals = []
            for i in range(j, j + 2):
                p = owner * per + i
                q = sector_from[p]
                totals.append(terms(q, p, hpsi[q]))
            for i in range(j, j + 2):
                if off:
                    zs2[off - 1, i] = totals[i - j].astype(BF16)
                    z2_copy(off, i).start()
                else:
                    z_own[i] = totals[i - j]

    def add_squares(q, sums):
        block = hpsi[q].astype(F32)
        return sums + block * block

    squares = lax.fori_loop(0, sectors, add_squares, jnp.zeros((block_len, block_len), F32))
    entries = sectors * block_len * block_len
    scale = lax.rsqrt(jnp.sum(squares, keepdims=True) / entries + 1e-06)
    for j in range(per):
        out1_ref[0, j] = hpsi[sector_from[first + j]]
    for j in range(per):
        total = z_own[j]
        for off in range(1, groups):
            z2_copy(off, j).wait_recv()
            total += zr2[off - 1, j].astype(F32)
        out2_ref[0, j] = (back(sector_from[first + j], total) * scale).astype(BF16)

    for off in range(1, segs):
        lab_copy(off, seg).wait_send()
    for off in range(1, groups):
        wave_copy(off, me).wait_send()
        for j in range(per):
            prefix_copy(off, j, me).wait_send()
            z1_copy(off, j).wait_send()
            h_copy(off, j, me).wait_send()
            z2_copy(off, j).wait_send()

    @pl.when(seg < segs - 1)
    def _():
        for j in range(per):
            chain_copy(j).wait_send()


def on_device(label_map, site_blocks, left_ops, right_ops, wavefunction):
    segs, groups = lax.axis_size("seg"), lax.axis_size("op")
    sectors, n = site_blocks.shape[1], site_blocks.shape[2]
    ops = left_ops.shape[0]
    per = sectors // groups
    dma = pltpu.SemaphoreType.DMA
    peers = groups - 1
    blocks = lambda *lead, dtype=BF16: pltpu.VMEM(lead + (n, n), dtype)
    out = jax.ShapeDtypeStruct((1, per, n, n), BF16)
    vmem = pl.BlockSpec(memory_space=pltpu.VMEM)
    hbm = pl.BlockSpec(memory_space=pl.ANY)
    return pl.pallas_call(
        functools.partial(kernel, segs, groups),
        out_shape=(out, out),
        in_specs=[vmem, hbm, hbm, hbm, hbm],
        out_specs=(vmem, vmem),
        scratch_shapes=[
            blocks(sectors, dtype=F32), blocks(ops, sectors), blocks(ops, sectors),
            blocks(sectors),
            pltpu.VMEM((8, 128), jnp.int32), pltpu.VMEM((segs, 8, 128), jnp.int32),
            pltpu.SMEM((segs, 8, 128), jnp.int32),
            pltpu.SMEM((sectors,), jnp.int32), pltpu.SMEM((sectors,), jnp.int32),
            blocks(sectors), blocks(per), blocks(per), blocks(per), blocks(sectors),
            blocks(per, dtype=F32),
            blocks(peers, per), blocks(peers, per), blocks(peers, per), blocks(peers, per),
            dma((4,)), dma, dma((segs - 1,)), dma((segs - 1,)), dma((peers,)), dma((peers,)),
            dma((per,)), dma((per,)),
            dma((peers, per)), dma((peers, per)), dma((peers, per)), dma((peers, per)),
            dma((peers, per)), dma((peers, per)), dma((peers, per)), dma((peers, per)),
        ],
        compiler_params=pltpu.CompilerParams(
            collective_id=0, has_side_effects=True, vmem_limit_bytes=56 * 1024 * 1024
        ),
    )(label_map, site_blocks, left_ops, right_ops, wavefunction)


def solution(mesh):
    in_specs = (
        P("seg", None),
        P("seg", None, None, None),
        P("op", None, None, None),
        P("seg", "op", None, None, None),
        P("seg", "op", None, None),
    )
    out_specs = (P("seg", "op", None, None), P("seg", "op", None, None))
    return jax.shard_map(
        on_device, mesh=mesh, in_specs=in_specs, out_specs=out_specs, check_vma=False
    )
```
